32 devices in a mesh: seq: 16 (over z, y, x), head: 2 (over core).
Axes of the slice: x: 2, y: 2, z: 4, core: 2. Of those that a mesh axis runs over, the one named last changes fastest.
Arguments:
- queries: bfloat16 [2048, 8192], P('seq', 'head'), may hold values from -6 to 6
- keys: bfloat16 [2048, 8192], P('seq', 'head'), may hold values from -6 to 6
- values: bfloat16 [2048, 8192], P('seq', 'head'), may hold values from -48 to 48, as said below
- cotangent: bfloat16 [2048, 8192], P('seq', 'head'), may hold values from -6 to 6
- gain: float32 [8192], P('head'), may hold values from 0.1 to 1.9
Outputs:
- query_grad: bfloat16 [2048, 8192], P('seq', 'head')
- key_grad: bfloat16 [2048, 8192], P('seq', 'head')
- value_grad: bfloat16 [2048, 8192], P('seq', 'head')
The draws below stay inside these ranges and needn't reach their ends.
Inputs may be any that keep to these rules, and one draw needn't show every extreme that they name: Real values.
All inputs are finite; a program needn't handle non-finite values.
Results may differ from the reference program's by a relative error of at most 0.0058.
Values sent between devices are 32-bit elements; how exact they have to be, the bound alone decides.
No kernel may reach another device: no remote copies, remote signals or barrier semaphores. Data moves between devices by JAX's collectives and lax.ppermute only.
A program may use at most 128 MiB of HBM per device.

```python
import math
import jax
import jax.numpy as jnp
from jax import lax

HEADS = 64
HEAD_DIM = 128
T_DEV = 128
SEQ_LEN = 2048
WIDTH = 8192
N_SEQ = 16


def draw_values(key, part):
    first, second, third = jax.random.split(jax.random.fold_in(key, 17), 3)
    position = jnp.arange(WIDTH).astype(jnp.float32) / WIDTH
    column_scale = jnp.exp(math.log(3.0) * position) * jnp.exp(jax.random.uniform(second, (WIDTH,), jnp.float32, 0.0, math.log(4.0)))
    row_scale = jnp.exp(jax.random.uniform(third, (SEQ_LEN, 1), jnp.float32, 0.0, math.log(10.0)))
    base = jnp.clip(jax.random.normal(first, (SEQ_LEN, WIDTH), jnp.float32), -4.0, 4.0)
    return (0.1 * base * row_scale * column_scale[None, :]).astype(jnp.bfloat16)


def block_scale(stream_key, extent, shards, low, high):
    factor_of = 1.0
    for axis_at, blocks in shards:
        draws = jax.random.uniform(jax.random.fold_in(jax.random.fold_in(stream_key, 6), axis_at), (blocks,), jnp.float32, low / len(shards), high / len(shards))
        factor_of = factor_of * jnp.repeat(jnp.exp(draws), extent[axis_at] // blocks).reshape((-1,) + (1,) * (len(extent) - 1 - axis_at))
    return factor_of


def bell_draw(key, dims, spread, bound, cuts=(), kind=jnp.bfloat16):
    loudness = block_scale(key, dims, cuts, -0.22, 0.18) if cuts else 1.0
    drawn = jax.random.normal(key, dims, jnp.float32) * spread * loudness
    return jnp.minimum(jnp.maximum(drawn, -bound), bound).astype(kind)


def setup_inputs(seed: int = 0) -> dict:
    streams_of = jax.random.split(jax.random.key(seed), 6)
    queries = bell_draw(streams_of[0], (SEQ_LEN, WIDTH), 1.0, 6.0, ((0, 16), (1, 2)))
    keys = bell_draw(streams_of[1], (SEQ_LEN, WIDTH), 1.0, 6.0, ((0, 16), (1, 2)))
    values = draw_values(jax.random.fold_in(streams_of[5], 71), 0)
    cotangent = bell_draw(streams_of[3], (SEQ_LEN, WIDTH), 1.0, 6.0, ((0, 16), (1, 2)))
    gain = jnp.clip(1.0 + 0.18 * jax.random.normal(streams_of[4], (WIDTH,), jnp.float32), 0.1, 1.9)
    return dict(queries=queries, keys=keys, values=values, cotangent=cotangent, gain=gain)


epsilon = 1e-05

def split_blocks(array):
    return array.reshape(N_SEQ, T_DEV, HEADS, HEAD_DIM).astype(jnp.float32)

def reference(queries, keys, values, cotangent, gain):
    score_scale = HEAD_DIM ** (-0.5)
    rows_index = lax.broadcasted_iota(jnp.int32, (T_DEV, T_DEV), 0)
    cols_index = lax.broadcasted_iota(jnp.int32, (T_DEV, T_DEV), 1)
    causal_mask = (rows_index >= cols_index)[None, :, :]
    query_blocks = split_blocks(queries)
    key_blocks = split_blocks(keys)
    value_blocks = split_blocks(values)

    def block_weights(query_block, key_block):
        scores = jnp.einsum('thd,shd->hts', query_block, key_block) * score_scale
        rounded = jnp.where(causal_mask, scores, 0.0).astype(jnp.bfloat16)
        return lax.optimization_barrier(rounded).astype(jnp.float32)

    def forward_step(state, inputs):
        query_block, key_block, value_block = inputs
        state_low = lax.optimization_barrier(state.astype(jnp.bfloat16)).astype(jnp.float32)
        weights = block_weights(query_block, key_block)
        attended = jnp.einsum('hts,shd->thd', weights, value_block)
        attended = attended + score_scale * jnp.einsum('thd,hde->the', query_block, state_low)
        new_state = state + jnp.einsum('shd,she->hde', key_block, value_block)
        return (new_state, (attended, state_low))
    start_state = jnp.zeros((HEADS, HEAD_DIM, HEAD_DIM), jnp.float32)
    final_state, outputs = lax.scan(forward_step, start_state, (query_blocks, key_blocks, value_blocks))
    attended_blocks, prefix_blocks = outputs
    attended = attended_blocks.reshape(SEQ_LEN, WIDTH)
    squares = lax.optimization_barrier(jnp.mean(attended * attended, axis=1))
    inverse_rms = lax.rsqrt(squares + epsilon)
    normed = attended * inverse_rms[:, None]
    scaled = cotangent.astype(jnp.float32) * gain[None, :]
    cross = lax.optimization_barrier(jnp.mean(scaled * normed, axis=1))
    grad_attended = ((scaled - normed * cross[:, None]) * inverse_rms[:, None]).astype(jnp.bfloat16)
    grad_blocks = split_blocks(grad_attended)

    def backward_step(state, inputs):
        query_block, key_block, value_block, grad_block, prefix_low = inputs
        suffix_low = lax.optimization_barrier(state.astype(jnp.bfloat16)).astype(jnp.float32)
        weights = block_weights(query_block, key_block)
        grad_scores = jnp.einsum('the,she->hts', grad_block, value_block) * score_scale
        grad_weights = jnp.where(causal_mask, grad_scores, 0.0).astype(jnp.bfloat16)
        grad_weights = lax.optimization_barrier(grad_weights).astype(jnp.float32)
        query_grad = jnp.einsum('hts,shd->thd', grad_weights, key_block)
        query_grad = query_grad + score_scale * jnp.einsum('the,hde->thd', grad_block, prefix_low)
        key_grad = jnp.einsum('hts,thd->shd', grad_weights, query_block)
        key_grad = key_grad + score_scale * jnp.einsum('she,hde->shd', value_block, suffix_low)
        value_grad = jnp.einsum('hts,the->she', weights, grad_block)
        value_grad = value_grad + score_scale * jnp.einsum('shd,hde->she', key_block, suffix_low)
        new_state = state + jnp.einsum('thd,the->hde', query_block, grad_block)
        return (new_state, (query_grad.astype(jnp.bfloat16), key_grad.astype(jnp.bfloat16), value_grad.astype(jnp.bfloat16)))
    last_state, grads = lax.scan(backward_step, start_state, (query_blocks, key_blocks, value_blocks, grad_blocks, prefix_blocks), reverse=True)
    query_grad, key_grad, value_grad = grads
    return (query_grad.reshape(SEQ_LEN, WIDTH), key_grad.reshape(SEQ_LEN, WIDTH), value_grad.reshape(SEQ_LEN, WIDTH))
```

```python
import functools
import math

import jax
import jax.numpy as jnp
from jax import lax
from jax.experimental import pallas as pl
from jax.experimental.pallas import tpu as pltpu
from jax.sharding import PartitionSpec as P

HEAD_DIM = 128
GROUPS = 2
PLANE = 4

epsilon = 1e-05

CONTRACT_ROWS = (((0,), (0,)), ((), ()))
CONTRACT_COLUMNS = (((1,), (1,)), ((), ()))


def dot(a, b, dims=(((1,), (0,)), ((), ()))):
    return lax.dot_general(a, b, dims, preferred_element_type=jnp.float32)


def call(body, outs, *args, flops=0, aliases=None):
    moved = sum(math.prod(a.shape) * a.dtype.itemsize for a in (*args, *outs))
    return pl.pallas_call(
        body,
        out_shape=outs,
        in_specs=[pl.BlockSpec(memory_space=pltpu.VMEM)] * len(args),
        out_specs=[pl.BlockSpec(memory_space=pltpu.VMEM)] * len(outs),
        input_output_aliases=aliases or {},
        cost_estimate=pl.CostEstimate(flops=flops, bytes_accessed=moved, transcendentals=0),
        compiler_params=pltpu.CompilerParams(vmem_limit_bytes=40 * 1024 * 1024),
    )(*args)


def f32(*shape):
    return jax.ShapeDtypeStruct(shape, jnp.float32)


def bf16(*shape):
    return jax.ShapeDtypeStruct(shape, jnp.bfloat16)


def place():
    me = lax.axis_index("seq")
    return lax.rem(me, PLANE), lax.div(me, PLANE)


def weight(condition):
    return jnp.where(condition, 1.0, 0.0).astype(jnp.float32)


def head_columns(group, owner, per_owner, j):
    return pl.ds(pl.multiple_of(((group * PLANE + owner) * per_owner + j) * HEAD_DIM, HEAD_DIM), HEAD_DIM)


def causal(tokens):
    rows_index = lax.broadcasted_iota(jnp.int32, (tokens, tokens), 0)
    cols_index = lax.broadcasted_iota(jnp.int32, (tokens, tokens), 1)
    return rows_index >= cols_index


def total_kernel(lines, *refs):
    parts, outs = refs[:PLANE], refs[PLANE:]
    _, z = place()
    rows = outs[0].shape[0]
    for k in range(lines):
        at = pl.ds(pl.multiple_of(lax.rem(z + k, lines) * rows, 8), rows)
        total = parts[0][at, :]
        for part in parts[1:]:
            total = total + part[at, :]
        outs[k][...] = total


def line_kernel(lines, reverse, *refs):
    pieces, outs = refs[:lines], refs[lines:]
    _, z = place()
    for k in range(lines):
        target = lax.rem(z + k, lines)
        total = None
        for j in range(lines):
            source = lax.rem(z + lines - j, lines)
            before = source > target if reverse else source < target
            term = pieces[j][...] * weight(before)
            total = term if total is None else total + term
        outs[k][...] = total


def spread_kernel(lines, reverse, *refs):
    entering, parts, outs = refs[:lines], refs[lines : lines + PLANE], refs[lines + PLANE :]
    p, z = place()
    rows = entering[0].shape[0]
    for i in range(lines):
        at = pl.ds(pl.multiple_of(lax.rem(z + lines - i, lines) * rows, 8), rows)
        base = entering[i][...]
        held = [part[at, :] for part in parts]
        for k in range(PLANE):
            target = p ^ k
            total = base
            for j in range(PLANE):
                source = p ^ j
                before = source > target if reverse else source < target
                total = total + held[j] * weight(before)
            outs[k][at, :] = total


def plane_send(parts):
    n = lax.axis_size("seq")
    return [parts[0]] + [
        lax.ppermute(parts[k], "seq", [(s, s ^ k) for s in range(n)]) for k in range(1, PLANE)
    ]


def line_send(pieces):
    n = lax.axis_size("seq")
    return [pieces[0]] + [
        lax.ppermute(pieces[k], "seq", [(s, (s + PLANE * k) % n) for s in range(n)])
        for k in range(1, len(pieces))
    ]


def line_scan_long(parts, reverse):
    n = lax.axis_size("seq")
    lines = n // PLANE
    z = lax.axis_index("seq") // PLANE
    total = sum(parts)
    groups = [[i + PLANE * l for l in range(lines)] for i in range(PLANE)]
    send = functools.partial(
        lax.all_to_all, axis_name="seq", split_axis=0, concat_axis=0, axis_index_groups=groups, tiled=True
    )
    every = send(total).reshape(lines, -1, HEAD_DIM)
    inclusive = lax.cumsum(every, axis=0, reverse=reverse)
    zero = jnp.zeros_like(every[:1])
    before = (
        jnp.concatenate([inclusive[1:], zero]) if reverse else jnp.concatenate([zero, inclusive[:-1]])
    )
    entering = send(before.reshape(total.shape)).reshape(lines, -1, HEAD_DIM)
    return [
        lax.dynamic_index_in_dim(entering, (z + lines - i) % lines, 0, keepdims=False) for i in range(lines)
    ]


def scan_states(groups, reverse):
    lines = lax.axis_size("seq") // PLANE
    rows = groups[0][0].shape[0]
    piece = rows // lines
    results = []
    for parts in groups:
        parts = plane_send(parts)
        if lines <= 4:
            pieces = call(functools.partial(total_kernel, lines), [f32(piece, HEAD_DIM)] * lines, *parts)
            pieces = line_send(pieces)
            pieces = call(functools.partial(line_kernel, lines, reverse), [f32(piece, HEAD_DIM)] * lines, *pieces)
            entering = line_send(pieces)
        else:
            entering = line_scan_long(parts, reverse)
        outs = call(
            functools.partial(spread_kernel, lines, reverse), [f32(rows, HEAD_DIM)] * PLANE, *entering, *parts
        )
        results.append(plane_send(outs))
    return results


def state_kernel(group, left, right, *outs):
    p, _ = place()
    per_owner = outs[0].shape[0] // HEAD_DIM
    for k in range(PLANE):
        for j in range(per_owner):
            at = head_columns(group, p ^ k, per_owner, j)
            outs[k][pl.ds(j * HEAD_DIM, HEAD_DIM), :] = dot(left[:, at], right[:, at], CONTRACT_ROWS)


def local_kernel(scale, queries, keys, values, weights, inner):
    mask = causal(queries.shape[0])
    for h in range(queries.shape[1] // HEAD_DIM):
        at = pl.ds(h * HEAD_DIM, HEAD_DIM)
        scores = dot(queries[:, at], keys[:, at], CONTRACT_COLUMNS) * scale
        w = jnp.where(mask, scores, 0.0).astype(jnp.bfloat16)
        weights[:, at] = w
        inner[:, at] = dot(w, values[:, at])


def attend_kernel(group, scale, queries, inner, cotangent, gain, *refs):
    parts, (attended, prefix_low, stats) = refs[:PLANE], refs[PLANE:]
    p, _ = place()
    per_owner = parts[0].shape[0] // HEAD_DIM
    squares = cross = None
    for k in range(PLANE):
        for j in range(per_owner):
            at = head_columns(group, p ^ k, per_owner, j)
            here = head_columns(0, p ^ k, per_owner, j)
            low = parts[k][pl.ds(j * HEAD_DIM, HEAD_DIM), :].astype(jnp.bfloat16)
            prefix_low[:, here] = low
            a = inner[:, at] + scale * dot(queries[:, at], low)
            attended[:, here] = a
            scaled = cotangent[:, at].astype(jnp.float32) * gain[:, at]
            squares = a * a if squares is None else squares + a * a
            cross = scaled * a if cross is None else cross + scaled * a
    stats[0] = squares
    stats[1] = cross


def grad_kernel(group, width, queries, cotangent, gain, stats, attended, grad, *outs):
    p, _ = place()
    per_owner = outs[0].shape[0] // HEAD_DIM
    inverse_rms = lax.rsqrt(jnp.sum(stats[0], axis=1, keepdims=True) / width + epsilon)
    cross = jnp.sum(stats[1], axis=1, keepdims=True) * inverse_rms / width
    for k in range(PLANE):
        for j in range(per_owner):
            at = head_columns(group, p ^ k, per_owner, j)
            here = head_columns(0, p ^ k, per_owner, j)
            normed = attended[:, here] * inverse_rms
            scaled = cotangent[:, at].astype(jnp.float32) * gain[:, at]
            g = ((scaled - normed * cross) * inverse_rms).astype(jnp.bfloat16)
            grad[:, here] = g
            outs[k][pl.ds(j * HEAD_DIM, HEAD_DIM), :] = dot(queries[:, at], g, CONTRACT_ROWS)


def local_grad_kernel(scale, *refs):
    queries, keys, values, weights = refs[:4]
    grads, lows = refs[4 : 4 + GROUPS], refs[4 + GROUPS : 4 + 2 * GROUPS]
    query_grad, key_inner, value_inner = refs[4 + 2 * GROUPS :]
    mask = causal(queries.shape[0])
    heads = queries.shape[1] // HEAD_DIM // GROUPS
    for h in range(heads * GROUPS):
        at = pl.ds(h * HEAD_DIM, HEAD_DIM)
        here = pl.ds((h % heads) * HEAD_DIM, HEAD_DIM)
        g = grads[h // heads][:, here]
        low = lows[h // heads][:, here]
        scores = dot(g, values[:, at], CONTRACT_COLUMNS) * scale
        gw = jnp.where(mask, scores, 0.0).astype(jnp.bfloat16)
        query = dot(gw, keys[:, at]) + scale * dot(g, low, CONTRACT_COLUMNS)
        query_grad[:, at] = query.astype(jnp.bfloat16)
        key_inner[:, at] = dot(gw, queries[:, at], CONTRACT_ROWS)
        value_inner[:, at] = dot(weights[:, at], g, CONTRACT_ROWS)


def finish_kernel(scale, keys, values, key_inner, value_inner, *refs):
    parts, (key_grad, value_grad) = refs[: PLANE * GROUPS], refs[PLANE * GROUPS :]
    p, _ = place()
    per_owner = parts[0].shape[0] // HEAD_DIM
    for group in range(GROUPS):
        for k in range(PLANE):
            for j in range(per_owner):
                at = head_columns(group, p ^ k, per_owner, j)
                low = parts[group * PLANE + k][pl.ds(j * HEAD_DIM, HEAD_DIM), :].astype(jnp.bfloat16)
                key = key_inner[:, at] + scale * dot(values[:, at], low, CONTRACT_COLUMNS)
                key_grad[:, at] = key.astype(jnp.bfloat16)
                value = value_inner[:, at] + scale * dot(keys[:, at], low)
                value_grad[:, at] = value.astype(jnp.bfloat16)


def per_device(queries, keys, values, cotangent, gain):
    tokens, width = queries.shape
    total_width = width * lax.axis_size("head")
    scale = HEAD_DIM ** (-0.5)
    share = width // GROUPS
    state = f32(share // PLANE, HEAD_DIM)
    product = 2 * tokens * width * HEAD_DIM
    gain = gain[None, :]

    with jax.named_scope("state"):
        states = [
            call(functools.partial(state_kernel, g), [state] * PLANE, keys, values, flops=product // GROUPS)
            for g in range(GROUPS)
        ]
    with jax.named_scope("prefix"):
        prefixes = scan_states(states, False)
    with jax.named_scope("local"):
        weights, inner = call(
            functools.partial(local_kernel, scale),
            [bf16(tokens, width), f32(tokens, width)],
            queries, keys, values, flops=2 * product,
        )
    with jax.named_scope("attend"):
        attended = [
            call(
                functools.partial(attend_kernel, g, scale),
                [f32(tokens, share), bf16(HEAD_DIM, share), f32(2, tokens, HEAD_DIM)],
                queries, inner, cotangent, gain, *prefixes[g], flops=product // GROUPS,
            )
            for g in range(GROUPS)
        ]
        stats = lax.psum(sum(a[2] for a in attended), "head")
    with jax.named_scope("grad"):
        grads = [
            call(
                functools.partial(grad_kernel, g, total_width),
                [bf16(tokens, share)] + [state] * PLANE,
                queries, cotangent, gain, stats, attended[g][0], flops=product // GROUPS,
            )
            for g in range(GROUPS)
        ]
    with jax.named_scope("suffix"):
        suffixes = scan_states([g[1:] for g in grads], True)
    with jax.named_scope("local_grad"):
        query_grad, key_inner, value_inner = call(
            functools.partial(local_grad_kernel, scale),
            [bf16(tokens, width), f32(tokens, width), f32(tokens, width)],
            queries, keys, values, weights, *[g[0] for g in grads], *[a[1] for a in attended],
            flops=5 * product,
        )
    with jax.named_scope("finish"):
        key_grad, value_grad = call(
            functools.partial(finish_kernel, scale),
            [bf16(tokens, width)] * 2,
            keys, values, key_inner, value_inner, *[s for group in suffixes for s in group],
            flops=2 * product,
        )
    return query_grad, key_grad, value_grad


def solution(mesh):
    return jax.shard_map(
        per_device,
        mesh=mesh,
        in_specs=(P("seq", "head"), P("seq", "head"), P("seq", "head"), P("seq", "head"), P("head")),
        out_specs=(P("seq", "head"), P("seq", "head"), P("seq", "head")),
        check_vma=False,
    )
```

```python
import functools
import math

import jax
import jax.numpy as jnp
from jax import lax
from jax.experimental import pallas as pl
from jax.experimental.pallas import tpu as pltpu
from jax.sharding import PartitionSpec as P

HEAD_DIM = 128
GROUPS = 2
HIDDEN = 4 * 10**9
PLANE = 4

epsilon = 1e-05

CONTRACT_ROWS = (((0,), (0,)), ((), ()))
CONTRACT_COLUMNS = (((1,), (1,)), ((), ()))


def dot(a, b, dims=(((1,), (0,)), ((), ()))):
    return lax.dot_general(a, b, dims, preferred_element_type=jnp.float32)


class Chain:
    def __init__(self):
        self.last = None

    def __call__(self, body, outs, *args, flops=1):
        specs = [pl.BlockSpec(memory_space=pltpu.VMEM)] * len(args)
        kernel, operands, count = body, args, len(args)
        if self.last is not None:
            specs, operands = specs + [pl.BlockSpec(memory_space=pl.ANY)], (*args, self.last)

            def kernel(*refs):
                body(*refs[:count], *refs[count + 1 :])

        results = pl.pallas_call(
            kernel,
            out_shape=outs,
            in_specs=specs,
            out_specs=[pl.BlockSpec(memory_space=pltpu.VMEM)] * len(outs),
            cost_estimate=pl.CostEstimate(flops=flops, bytes_accessed=1, transcendentals=0),
            compiler_params=pltpu.CompilerParams(vmem_limit_bytes=16 * 1024 * 1024),
        )(*operands)
        self.last = results[-1]
        return results


def f32(*shape):
    return jax.ShapeDtypeStruct(shape, jnp.float32)


def bf16(*shape):
    return jax.ShapeDtypeStruct(shape, jnp.bfloat16)


def place():
    me = lax.axis_index("seq")
    return lax.rem(me, PLANE), lax.div(me, PLANE)


def weight(condition):
    return jnp.where(condition, 1.0, 0.0).astype(jnp.float32)


def head_columns(group, owner, per_owner, j):
    return pl.ds(pl.multiple_of(((group * PLANE + owner) * per_owner + j) * HEAD_DIM, HEAD_DIM), HEAD_DIM)


def causal(tokens):
    rows_index = lax.broadcasted_iota(jnp.int32, (tokens, tokens), 0)
    cols_index = lax.broadcasted_iota(jnp.int32, (tokens, tokens), 1)
    return rows_index >= cols_index


def exchange(value, distance):
    n = lax.axis_size("seq")
    return lax.ppermute(value, "seq", [(s, s ^ distance) for s in range(n)])


def plane_send(parts):
    return [parts[0]] + [exchange(parts[k], k) for k in range(1, PLANE)]


def bit(level):
    _, z = place()
    return lax.rem(lax.div(z, 1 << level), 2)


def half(side, rows):
    return pl.ds(pl.multiple_of(side * rows, 8), rows)


def total_kernel(level, *refs):
    parts, outs = refs[:-2], refs[-2:]
    rows = outs[0].shape[0]
    side = bit(level)
    for out, at in zip(outs, (half(side, rows), half(1 - side, rows))):
        total = parts[0][at, :]
        for part in parts[1:]:
            total = total + part[at, :]
        out[...] = total


def sum_kernel(*refs):
    total = refs[0][...]
    for part in refs[1:-1]:
        total = total + part[...]
    refs[-1][...] = total


def first(level, reverse):
    later = bit(level).astype(jnp.float32)
    return (1.0 - later, later) if reverse else (later, 1.0 - later)


def edge_kernel(level, reverse, other, mine, theirs, to_me, to_partner):
    entering = other[...] * first(level + 1, reverse)[0]
    before_me, before_partner = first(level, reverse)
    to_me[...] = entering + theirs[...] * before_me
    to_partner[...] = entering + mine[...] * before_partner


def inner_kernel(level, reverse, kept, received, mine, theirs, to_me, to_partner):
    rows = kept.shape[0]
    side = bit(level + 1)
    before_me, before_partner = first(level, reverse)
    for entering, at in ((kept, half(side, rows)), (received, half(1 - side, rows))):
        to_me[at, :] = entering[...] + theirs[at, :] * before_me
        to_partner[at, :] = entering[...] + mine[at, :] * before_partner


def spread_kernel(reverse, kept, received, *refs):
    parts, outs = refs[:PLANE], refs[PLANE:]
    p, _ = place()
    rows = kept.shape[0]
    side = bit(0)
    for base, at in ((kept, half(side, rows)), (received, half(1 - side, rows))):
        held = [part[at, :] for part in parts]
        for k in range(PLANE):
            target = p ^ k
            total = base[...]
            for j in range(PLANE):
                source = p ^ j
                before = source > target if reverse else source < target
                total = total + held[j] * weight(before)
            outs[k][at, :] = total


def line_steps(run, parts, reverse, level=0):
    levels = (lax.axis_size("seq") // PLANE).bit_length() - 1
    distance = PLANE << level
    rows = parts[0].shape[0] // 2
    mine, send = run(functools.partial(total_kernel, level), [f32(rows, HEAD_DIM)] * 2, *parts)
    theirs = exchange(send, distance)
    yield
    if level == levels - 2:
        (total,) = run(sum_kernel, [f32(rows, HEAD_DIM)], mine, theirs)
        entering = (exchange(total, 2 * distance),)
        body = edge_kernel
        yield
    else:
        entering = yield from line_steps(run, (mine, theirs), reverse, level + 1)
        body = inner_kernel
    kept, send = run(
        functools.partial(body, level, reverse), [f32(rows, HEAD_DIM)] * 2, *entering, mine, theirs
    )
    received = exchange(send, distance)
    yield
    return kept, received


def scan_steps(run, parts, reverse, results):
    parts = plane_send(parts)
    yield
    kept, received = yield from line_steps(run, parts, reverse)
    rows = parts[0].shape[0]
    outs = run(
        functools.partial(spread_kernel, reverse), [f32(rows, HEAD_DIM)] * PLANE, kept, received, *parts
    )
    results.append(plane_send(outs))


def scan_states(run, groups, reverse):
    results = []
    steps = [scan_steps(run, parts, reverse, results) for parts in groups]
    for one in steps:
        next(one)
    time, ended = 0, set()
    while len(ended) < len(steps):
        for g, one in reversed(list(enumerate(steps))):
            if g not in ended and time >= 2 * g:
                try:
                    next(one)
                except StopIteration:
                    ended.add(g)
        time += 1
    return results


def state_kernel(group, left, right, *outs):
    p, _ = place()
    per_owner = outs[0].shape[0] // HEAD_DIM
    for k in range(PLANE):
        for j in range(per_owner):
            at = head_columns(group, p ^ k, per_owner, j)
            outs[k][pl.ds(j * HEAD_DIM, HEAD_DIM), :] = dot(left[:, at], right[:, at], CONTRACT_ROWS)


def local_kernel(scale, queries, keys, values, weights, inner):
    mask = causal(queries.shape[0])
    for h in range(queries.shape[1] // HEAD_DIM):
        at = pl.ds(h * HEAD_DIM, HEAD_DIM)
        scores = dot(queries[:, at], keys[:, at], CONTRACT_COLUMNS) * scale
        w = jnp.where(mask, scores, 0.0).astype(jnp.bfloat16)
        weights[:, at] = w
        inner[:, at] = dot(w, values[:, at])


def attend_kernel(group, scale, queries, inner, cotangent, gain, *refs):
    parts, (attended, prefix_low, stats) = refs[:PLANE], refs[-3:]
    earlier = refs[PLANE:-3]
    p, _ = place()
    per_owner = parts[0].shape[0] // HEAD_DIM
    squares, cross = (earlier[0][0], earlier[0][1]) if earlier else (0.0, 0.0)
    for k in range(PLANE):
        for j in range(per_owner):
            at = head_columns(group, p ^ k, per_owner, j)
            here = head_columns(0, p ^ k, per_owner, j)
            low = parts[k][pl.ds(j * HEAD_DIM, HEAD_DIM), :].astype(jnp.bfloat16)
            prefix_low[:, here] = low
            a = inner[:, at] + scale * dot(queries[:, at], low)
            attended[:, here] = a
            scaled = cotangent[:, at].astype(jnp.float32) * gain[:, at]
            squares = squares + a * a
            cross = cross + scaled * a
    stats[0] = squares
    stats[1] = cross


def grad_kernel(group, width, queries, cotangent, gain, attended, *refs):
    p, _ = place()
    stats, (grad, *outs) = refs[: -PLANE - 1], refs[-PLANE - 1 :]
    per_owner = outs[0].shape[0] // HEAD_DIM
    squares, cross = stats[0][0], stats[0][1]
    for other in stats[1:]:
        squares, cross = squares + other[0], cross + other[1]
    inverse_rms = lax.rsqrt(jnp.sum(squares, axis=1, keepdims=True) / width + epsilon)
    cross = jnp.sum(cross, axis=1, keepdims=True) * inverse_rms / width
    for k in range(PLANE):
        for j in range(per_owner):
            at = head_columns(group, p ^ k, per_owner, j)
            here = head_columns(0, p ^ k, per_owner, j)
            normed = attended[:, here] * inverse_rms
            scaled = cotangent[:, at].astype(jnp.float32) * gain[:, at]
            g = ((scaled - normed * cross) * inverse_rms).astype(jnp.bfloat16)
            grad[:, here] = g
            outs[k][pl.ds(j * HEAD_DIM, HEAD_DIM), :] = dot(queries[:, at], g, CONTRACT_ROWS)


def local_grad_kernel(scale, *refs):
    queries, keys, values, weights = refs[:4]
    grads, lows = refs[4 : 4 + GROUPS], refs[4 + GROUPS : 4 + 2 * GROUPS]
    query_grad, key_inner, value_inner = refs[4 + 2 * GROUPS :]
    mask = causal(queries.shape[0])
    heads = queries.shape[1] // HEAD_DIM // GROUPS
    for h in range(heads * GROUPS):
        at = pl.ds(h * HEAD_DIM, HEAD_DIM)
        here = pl.ds((h % heads) * HEAD_DIM, HEAD_DIM)
        g = grads[h // heads][:, here]
        low = lows[h // heads][:, here]
        scores = dot(g, values[:, at], CONTRACT_COLUMNS) * scale
        gw = jnp.where(mask, scores, 0.0).astype(jnp.bfloat16)
        query = dot(gw, keys[:, at]) + scale * dot(g, low, CONTRACT_COLUMNS)
        query_grad[:, at] = query.astype(jnp.bfloat16)
        key_inner[:, at] = dot(gw, queries[:, at], CONTRACT_ROWS)
        value_inner[:, at] = dot(weights[:, at], g, CONTRACT_ROWS)


def finish_kernel(group, scale, keys, values, key_inner, value_inner, *refs):
    parts, (key_grad, value_grad) = refs[:PLANE], refs[-2:]
    p, _ = place()
    per_owner = parts[0].shape[0] // HEAD_DIM
    base = group if key_grad.shape == keys.shape else 0
    earlier = refs[PLANE:-2]
    share = per_owner * PLANE * HEAD_DIM
    for g in range(len(earlier) // 2):
        key_grad[:, pl.ds(g * share, share)] = earlier[2 * g][...]
        value_grad[:, pl.ds(g * share, share)] = earlier[2 * g + 1][...]
    for k in range(PLANE):
        for j in range(per_owner):
            at = head_columns(group, p ^ k, per_owner, j)
            there = head_columns(base, p ^ k, per_owner, j)
            low = parts[k][pl.ds(j * HEAD_DIM, HEAD_DIM), :].astype(jnp.bfloat16)
            key = key_inner[:, at] + scale * dot(values[:, at], low, CONTRACT_COLUMNS)
            key_grad[:, there] = key.astype(jnp.bfloat16)
            value = value_inner[:, at] + scale * dot(keys[:, at], low)
            value_grad[:, there] = value.astype(jnp.bfloat16)


def per_device(queries, keys, values, cotangent, gain):
    tokens, width = queries.shape
    ways = lax.axis_size("head")
    scale = HEAD_DIM ** (-0.5)
    share = width // GROUPS
    state = f32(share // PLANE, HEAD_DIM)
    gain = gain[None, :]
    run = Chain()

    with jax.named_scope("state"):
        states = [
            run(functools.partial(state_kernel, g), [state] * PLANE, keys, values)
            for g in range(GROUPS)
        ]
    with jax.named_scope("local"):
        weights, inner = run(
            functools.partial(local_kernel, scale),
            [bf16(tokens, width), f32(tokens, width)],
            queries, keys, values,
        )
    with jax.named_scope("prefix"):
        prefixes = scan_states(run, states, False)
    with jax.named_scope("attend"):
        attended = []
        for g in range(GROUPS):
            attended.append(
                run(
                    functools.partial(attend_kernel, g, scale),
                    [f32(tokens, share), bf16(HEAD_DIM, share), f32(2, tokens, HEAD_DIM)],
                    queries, inner, cotangent, gain, *prefixes[g], *[a[2] for a in attended[-1:]],
                    flops=HIDDEN if g < GROUPS - 1 else 1,
                )
            )
        stats = [attended[-1][2]]
        for k in range(1, ways):
            stats.append(lax.ppermute(stats[0], "head", [(h, (h + k) % ways) for h in range(ways)]))
    with jax.named_scope("grad"):
        grads = [
            run(
                functools.partial(grad_kernel, g, width * ways),
                [bf16(tokens, share)] + [state] * PLANE,
                queries, cotangent, gain, attended[g][0], *stats,
            )
            for g in range(GROUPS)
        ]
    with jax.named_scope("local_grad"):
        query_grad, key_inner, value_inner = run(
            functools.partial(local_grad_kernel, scale),
            [bf16(tokens, width), f32(tokens, width), f32(tokens, width)],
            queries, keys, values, weights, *[g[0] for g in grads], *[a[1] for a in attended],
        )
    with jax.named_scope("suffix"):
        suffixes = scan_states(run, [g[1:] for g in grads], True)
    with jax.named_scope("finish"):
        done = []
        for g in range(GROUPS):
            last = g == GROUPS - 1
            done += run(
                functools.partial(finish_kernel, g, scale),
                [bf16(tokens, width if last else share)] * 2,
                keys, values, key_inner, value_inner, *suffixes[g], *(done if last else []),
                flops=1 if last else HIDDEN,
            )
        key_grad, value_grad = done[-2:]
    return query_grad, key_grad, value_grad


def solution(mesh):
    return jax.shard_map(
        per_device,
        mesh=mesh,
        in_specs=(P("seq", "head"), P("seq", "head"), P("seq", "head"), P("seq", "head"), P("head")),
        out_specs=(P("seq", "head"), P("seq", "head"), P("seq", "head")),
        check_vma=False,
    )
```

```python
import functools

import jax
import jax.numpy as jnp
from jax import lax
from jax.experimental import pallas as pl
from jax.experimental.pallas import tpu as pltpu
from jax.sharding import PartitionSpec as P

HEAD_DIM = 128
GROUPS = 3
HIDDEN = 4 * 10**9
PLANE = 4

epsilon = 1e-05

CONTRACT_ROWS = (((0,), (0,)), ((), ()))
CONTRACT_COLUMNS = (((1,), (1,)), ((), ()))


def dot(a, b, dims=(((1,), (0,)), ((), ()))):
    return lax.dot_general(a, b, dims, preferred_element_type=jnp.float32)


class Chain:
    def __init__(self):
        self.last = None

    def __call__(self, body, outs, *args, flops=1, hbm_args=(), hbm_outs=0, aliases=None, scratch=()):
        specs = [pl.BlockSpec(memory_space=pltpu.HBM if i in hbm_args else pltpu.VMEM) for i in range(len(args))]
        kernel, operands, count = body, args, len(args)
        if self.last is not None and not any(self.last is arg for arg in args):
            specs, operands = specs + [pl.BlockSpec(memory_space=pl.ANY)], (*args, self.last)

            def kernel(*refs):
                body(*refs[:count], *refs[count + 1 :])

        results = pl.pallas_call(
            kernel,
            out_shape=outs,
            in_specs=specs,
            out_specs=[
                pl.BlockSpec(memory_space=pltpu.HBM if i < hbm_outs else pltpu.VMEM) for i in range(len(outs))
            ],
            scratch_shapes=scratch,
            input_output_aliases=aliases or {},
            cost_estimate=pl.CostEstimate(flops=flops, bytes_accessed=1, transcendentals=0),
            compiler_params=pltpu.CompilerParams(vmem_limit_bytes=16 * 1024 * 1024),
        )(*operands)
        self.last = results[-1]
        return results


def f32(*shape):
    return jax.ShapeDtypeStruct(shape, jnp.float32)


def bf16(*shape):
    return jax.ShapeDtypeStruct(shape, jnp.bfloat16)


def place():
    me = lax.axis_index("seq")
    return lax.rem(me, PLANE), lax.div(me, PLANE)


def weight(condition):
    return jnp.where(condition, 1.0, 0.0).astype(jnp.float32)


def columns(head, count=1):
    return pl.ds(pl.multiple_of(head * HEAD_DIM, HEAD_DIM), count * HEAD_DIM)


def split_heads(heads):
    per_owner = heads // PLANE
    groups = min(GROUPS, per_owner)
    sizes = [per_owner // groups + (g < per_owner % groups) for g in range(groups)]
    return [(PLANE * sum(sizes[:g]), sizes[g]) for g in range(groups)]


def causal(tokens):
    rows_index = lax.broadcasted_iota(jnp.int32, (tokens, tokens), 0)
    cols_index = lax.broadcasted_iota(jnp.int32, (tokens, tokens), 1)
    return rows_index >= cols_index


def exchange(value, distance):
    n = lax.axis_size("seq")
    return lax.ppermute(value, "seq", [(s, s ^ distance) for s in range(n)])


def plane_send(parts):
    return [parts[0]] + [exchange(parts[k], k) for k in range(1, PLANE)]


def bit(level):
    _, z = place()
    return lax.rem(lax.div(z, 1 << level), 2)


def half(side, rows):
    return pl.ds(pl.multiple_of(side * rows, 8), rows)


def total_kernel(level, *refs):
    parts, outs = refs[:-2], refs[-2:]
    rows = outs[0].shape[0]
    side = bit(level)
    for out, at in zip(outs, (half(side, rows), half(1 - side, rows))):
        total = parts[0][at, :]
        for part in parts[1:]:
            total = total + part[at, :]
        out[...] = total


def sum_kernel(*refs):
    total = refs[0][...]
    for part in refs[1:-1]:
        total = total + part[...]
    refs[-1][...] = total


def first(level, reverse):
    later = bit(level).astype(jnp.float32)
    return (1.0 - later, later) if reverse else (later, 1.0 - later)


def edge_kernel(level, reverse, other, mine, theirs, to_me, to_partner):
    entering = other[...] * first(level + 1, reverse)[0]
    before_me, before_partner = first(level, reverse)
    to_me[...] = entering + theirs[...] * before_me
    to_partner[...] = entering + mine[...] * before_partner


def inner_kernel(level, reverse, kept, received, mine, theirs, to_me, to_partner):
    rows = kept.shape[0]
    side = bit(level + 1)
    before_me, before_partner = first(level, reverse)
    for entering, at in ((kept, half(side, rows)), (received, half(1 - side, rows))):
        to_me[at, :] = entering[...] + theirs[at, :] * before_me
        to_partner[at, :] = entering[...] + mine[at, :] * before_partner


def spread_kernel(reverse, kept, received, *refs):
    parts, outs = refs[:PLANE], refs[PLANE:]
    p, _ = place()
    rows = kept.shape[0]
    side = bit(0)
    for base, at in ((kept, half(side, rows)), (received, half(1 - side, rows))):
        held = [part[at, :] for part in parts]
        for k in range(PLANE):
            target = p ^ k
            total = base[...]
            for j in range(PLANE):
                source = p ^ j
                before = source > target if reverse else source < target
                total = total + held[j] * weight(before)
            outs[k][at, :] = total


def line_steps(run, parts, reverse, level=0):
    levels = (lax.axis_size("seq") // PLANE).bit_length() - 1
    distance = PLANE << level
    rows = parts[0].shape[0] // 2
    mine, send = run(functools.partial(total_kernel, level), [f32(rows, HEAD_DIM)] * 2, *parts)
    theirs = exchange(send, distance)
    yield
    if level == levels - 2:
        (total,) = run(sum_kernel, [f32(rows, HEAD_DIM)], mine, theirs)
        entering = (exchange(total, 2 * distance),)
        body = edge_kernel
        yield
    else:
        entering = yield from line_steps(run, (mine, theirs), reverse, level + 1)
        body = inner_kernel
    kept, send = run(
        functools.partial(body, level, reverse), [f32(rows, HEAD_DIM)] * 2, *entering, mine, theirs
    )
    received = exchange(send, distance)
    yield
    return kept, received


def scan_steps(run, parts, reverse, results):
    parts = plane_send(parts)
    yield
    kept, received = yield from line_steps(run, parts, reverse)
    rows = parts[0].shape[0]
    outs = run(
        functools.partial(spread_kernel, reverse), [f32(rows, HEAD_DIM)] * PLANE, kept, received, *parts
    )
    results.append(plane_send(outs))


def scan_states(run, groups, reverse, fillers, use):
    results = []
    steps = [scan_steps(run, parts, reverse, results) for parts in groups]
    count = 2 * ((lax.axis_size("seq") // PLANE).bit_length() - 1)
    events = [(-1.0 if g == 0 else 1.0 + g / 10, filler) for g, filler in enumerate(fillers)]
    for g, one in enumerate(steps):
        next(one)
        behind = 0.5 + 1.2 * g if g else 0.0
        events += [(behind + step, functools.partial(next, one, None)) for step in range(count)]
        events.append((behind + count + 1, lambda g=g: use(g, results[g])))
    for _, event in sorted(events, key=lambda e: e[0]):
        event()


def state_of(first, count, p, left, right, outs):
    for k in range(PLANE):
        for j in range(count):
            at = columns(first + (p ^ k) * count + j)
            outs[k][pl.ds(j * HEAD_DIM, HEAD_DIM), :] = dot(left[:, at], right[:, at], CONTRACT_ROWS)


def first_state_kernel(first, count, keys, values, *refs):
    outs, (left, right, sems) = refs[:PLANE], refs[PLANE:]
    here = pl.ds(first * HEAD_DIM, PLANE * count * HEAD_DIM)
    copies = [
        pltpu.make_async_copy(source.at[:, here], target, sems.at[i])
        for i, (source, target) in enumerate(((keys, left), (values, right)))
    ]
    for copy in copies:
        copy.start()
    for copy in copies:
        copy.wait()
    state_of(0, count, place()[0], left, right, outs)


def state_kernel(first, count, keys, values, *outs):
    state_of(first, count, place()[0], keys, values, outs)


def local_kernel(first, scale, queries, keys, values, weights, inner):
    mask = causal(queries.shape[0])
    for h in range(inner.shape[1] // HEAD_DIM):
        at, here = columns(first + h), columns(h)
        scores = dot(queries[:, at], keys[:, at], CONTRACT_COLUMNS) * scale
        w = jnp.where(mask, scores, 0.0).astype(jnp.bfloat16)
        weights[:, here] = w
        inner[:, here] = dot(w, values[:, at])


def attend_kernel(first, count, scale, queries, inner, cotangent, gain, *refs):
    parts, (attended, prefix_low, stats) = refs[:PLANE], refs[-3:]
    earlier = refs[PLANE:-3]
    p, _ = place()
    squares, cross = (earlier[0][0], earlier[0][1]) if earlier else (0.0, 0.0)
    for k in range(PLANE):
        for j in range(count):
            h = (p ^ k) * count + j
            at, here = columns(first + h), columns(h)
            low = parts[k][pl.ds(j * HEAD_DIM, HEAD_DIM), :].astype(jnp.bfloat16)
            prefix_low[:, here] = low
            a = inner[:, here] + scale * dot(queries[:, at], low)
            attended[:, here] = a
            scaled = cotangent[:, at].astype(jnp.float32) * gain[:, at]
            squares = squares + a * a
            cross = cross + scaled * a
    stats[0] = squares
    stats[1] = cross


def grad_kernel(first, count, width, queries, cotangent, gain, attended, *refs):
    p, _ = place()
    stats, (grad, *outs) = refs[: -PLANE - 1], refs[-PLANE - 1 :]
    squares, cross = stats[0][0], stats[0][1]
    for other in stats[1:]:
        squares, cross = squares + other[0], cross + other[1]
    inverse_rms = lax.rsqrt(jnp.sum(squares, axis=1, keepdims=True) / width + epsilon)
    cross = jnp.sum(cross, axis=1, keepdims=True) * inverse_rms / width
    for k in range(PLANE):
        for j in range(count):
            h = (p ^ k) * count + j
            at, here = columns(first + h), columns(h)
            normed = attended[:, here] * inverse_rms
            scaled = cotangent[:, at].astype(jnp.float32) * gain[:, at]
            g = ((scaled - normed * cross) * inverse_rms).astype(jnp.bfloat16)
            grad[:, here] = g
            outs[k][pl.ds(j * HEAD_DIM, HEAD_DIM), :] = dot(queries[:, at], g, CONTRACT_ROWS)


def local_grad_kernel(first, scale, queries, keys, values, weights, grad, prefix_low, *refs):
    query_grad, key_inner, value_inner, query_block, sem = refs[-5:]
    mask = causal(queries.shape[0])
    heads = grad.shape[1] // HEAD_DIM
    for h in range(heads):
        at, here = columns(first + h), columns(h)
        g = grad[:, here]
        scores = dot(g, values[:, at], CONTRACT_COLUMNS) * scale
        gw = jnp.where(mask, scores, 0.0).astype(jnp.bfloat16)
        query = dot(gw, keys[:, at]) + scale * dot(g, prefix_low[:, here], CONTRACT_COLUMNS)
        query_block[:, here] = query.astype(jnp.bfloat16)
        key_inner[:, here] = dot(gw, queries[:, at], CONTRACT_ROWS)
        value_inner[:, here] = dot(weights[:, here], g, CONTRACT_ROWS)
    copy = pltpu.make_async_copy(query_block, query_grad.at[:, pl.ds(first * HEAD_DIM, heads * HEAD_DIM)], sem.at[0])
    copy.start()
    copy.wait()


def finish_kernel(first, count, scale, keys, values, key_inner, value_inner, *refs):
    parts, (key_grad, value_grad, key_block, value_block, sems) = refs[:PLANE], refs[-5:]
    p, _ = place()
    copies = []
    for k in range(PLANE):
        owner = (p ^ k) * count
        for j in range(count):
            at, here = columns(first + owner + j), columns(owner + j)
            low = parts[k][pl.ds(j * HEAD_DIM, HEAD_DIM), :].astype(jnp.bfloat16)
            key = key_inner[:, here] + scale * dot(values[:, at], low, CONTRACT_COLUMNS)
            key_block[:, here] = key.astype(jnp.bfloat16)
            value = value_inner[:, here] + scale * dot(keys[:, at], low)
            value_block[:, here] = value.astype(jnp.bfloat16)
        for i, (block, result) in enumerate(((key_block, key_grad), (value_block, value_grad))):
            copies.append(
                pltpu.make_async_copy(
                    block.at[:, columns(owner, count)],
                    result.at[:, columns(first + owner, count)],
                    sems.at[2 * k + i],
                )
            )
            copies[-1].start()
    for copy in copies:
        copy.wait()


def per_device(queries, keys, values, cotangent, gain):
    tokens, width = queries.shape
    ways = lax.axis_size("head")
    scale = HEAD_DIM ** (-0.5)
    gain = gain[None, :]
    groups = split_heads(width // HEAD_DIM)
    shares = [PLANE * count * HEAD_DIM for _, count in groups]
    states_of = [[f32(count * HEAD_DIM, HEAD_DIM)] * PLANE for _, count in groups]
    final = len(groups) - 1
    run = Chain()

    def block(g):
        return pltpu.VMEM((tokens, shares[g]), jnp.bfloat16)

    with jax.named_scope("state"):
        states = []
        for g, (first, count) in enumerate(groups):
            states.append(
                run(
                    functools.partial(state_kernel if g else first_state_kernel, first, count),
                    states_of[g], keys, values,
                    hbm_args=() if g else (0, 1),
                    scratch=[] if g else [block(0), block(0), pltpu.SemaphoreType.DMA((2,))],
                )
            )

    local, attended, local_grads, ends = [], [], [], []

    def run_local(g):
        local.append(
            run(
                functools.partial(local_kernel, groups[g][0], scale),
                [bf16(tokens, shares[g]), f32(tokens, shares[g])],
                queries, keys, values,
            )
        )

    def attend(g, prefix):
        attended.append(
            run(
                functools.partial(attend_kernel, *groups[g], scale),
                [f32(tokens, shares[g]), bf16(HEAD_DIM, shares[g]), f32(2, tokens, HEAD_DIM)],
                queries, local[g][1], cotangent, gain, *prefix, *[a[2] for a in attended[-1:]],
                flops=1 if g == final else HIDDEN,
            )
        )

    with jax.named_scope("prefix"):
        scan_states(run, states, False, [functools.partial(run_local, g) for g in range(final + 1)], attend)
    with jax.named_scope("statistics"):
        stats = [attended[-1][2]]
        for k in range(1, ways):
            stats.append(lax.ppermute(stats[0], "head", [(h, (h + k) % ways) for h in range(ways)]))
    with jax.named_scope("grad"):
        grads = [
            run(
                functools.partial(grad_kernel, first, count, width * ways),
                [bf16(tokens, shares[g])] + states_of[g],
                queries, cotangent, gain, attended[g][0], *stats,
            )
            for g, (first, count) in enumerate(groups)
        ]

    def run_local_grad(g):
        earlier = [r[0] for r in local_grads[-1:]]
        local_grads.append(
            run(
                functools.partial(local_grad_kernel, groups[g][0], scale),
                [bf16(tokens, width), f32(tokens, shares[g]), f32(tokens, shares[g])],
                queries, keys, values, local[g][0], grads[g][0], attended[g][1], *earlier,
                hbm_args=(6,), hbm_outs=1, aliases={6: 0} if earlier else {},
                scratch=[block(g), pltpu.SemaphoreType.DMA((1,))],
            )
        )

    def finish(g, suffix):
        at = 4 + PLANE
        earlier = ends[-1] if ends else []
        ends.append(
            run(
                functools.partial(finish_kernel, *groups[g], scale),
                [bf16(tokens, width)] * 2,
                keys, values, local_grads[g][1], local_grads[g][2], *suffix, *earlier,
                flops=1 if g == final else HIDDEN,
                hbm_args=(at, at + 1), hbm_outs=2, aliases={at: 0, at + 1: 1} if earlier else {},
                scratch=[block(g), block(g), pltpu.SemaphoreType.DMA((2 * PLANE,))],
            )
        )

    with jax.named_scope("suffix"):
        scan_states(
            run, [g[1:] for g in grads], True, [functools.partial(run_local_grad, g) for g in range(final + 1)], finish
        )
    return local_grads[-1][0], *ends[-1]


def solution(mesh):
    return jax.shard_map(
        per_device,
        mesh=mesh,
        in_specs=(P("seq", "head"), P("seq", "head"), P("seq", "head"), P("seq", "head"), P("head")),
        out_specs=(P("seq", "head"), P("seq", "head"), P("seq", "head")),
        check_vma=False,
    )
```

```python
import functools

import jax
import jax.numpy as jnp
from jax import lax
from jax.experimental import pallas as pl
from jax.experimental.pallas import tpu as pltpu
from jax.sharding import PartitionSpec as P

HEAD_DIM = 128
GROUPS = 2
HIDDEN = 4 * 10**9
PLANE = 4

epsilon = 1e-05

CONTRACT_ROWS = (((0,), (0,)), ((), ()))
CONTRACT_COLUMNS = (((1,), (1,)), ((), ()))


def dot(a, b, dims=(((1,), (0,)), ((), ()))):
    return lax.dot_general(a, b, dims, preferred_element_type=jnp.float32)


class Chain:
    def __init__(self):
        self.last = None

    def __call__(self, body, outs, *args, flops=1, hbm_args=(), hbm_outs=0, aliases=None, scratch=(), mib=16):
        specs = [pl.BlockSpec(memory_space=pltpu.HBM if i in hbm_args else pltpu.VMEM) for i in range(len(args))]
        kernel, operands, count = body, args, len(args)
        if self.last is not None and not any(self.last is arg for arg in args):
            specs, operands = specs + [pl.BlockSpec(memory_space=pl.ANY)], (*args, self.last)

            def kernel(*refs):
                body(*refs[:count], *refs[count + 1 :])

        results = pl.pallas_call(
            kernel,
            out_shape=outs,
            in_specs=specs,
            out_specs=[
                pl.BlockSpec(memory_space=pltpu.HBM if i < hbm_outs else pltpu.VMEM) for i in range(len(outs))
            ],
            scratch_shapes=scratch,
            input_output_aliases=aliases or {},
            cost_estimate=pl.CostEstimate(flops=flops, bytes_accessed=1, transcendentals=0),
            compiler_params=pltpu.CompilerParams(vmem_limit_bytes=mib * 1024 * 1024),
        )(*operands)
        self.last = results[-1]
        return list(results)


def f32(*shape):
    return jax.ShapeDtypeStruct(shape, jnp.float32)


def bf16(*shape):
    return jax.ShapeDtypeStruct(shape, jnp.bfloat16)


def place():
    me = lax.axis_index("seq")
    return lax.rem(me, PLANE), lax.div(me, PLANE)


def weight(condition):
    return jnp.where(condition, 1.0, 0.0).astype(jnp.float32)


def columns(head, count=1):
    return pl.ds(pl.multiple_of(head * HEAD_DIM, HEAD_DIM), count * HEAD_DIM)


def split_heads(heads):
    per_owner = heads // PLANE
    groups = min(GROUPS, per_owner)
    sizes = [per_owner // groups + (g < per_owner % groups) for g in range(groups)]
    return [(PLANE * sum(sizes[:g]), sizes[g]) for g in range(groups)]


def causal(tokens):
    rows_index = lax.broadcasted_iota(jnp.int32, (tokens, tokens), 0)
    cols_index = lax.broadcasted_iota(jnp.int32, (tokens, tokens), 1)
    return rows_index >= cols_index


def exchange(value, distance):
    n = lax.axis_size("seq")
    return lax.ppermute(value, "seq", [(s, s ^ distance) for s in range(n)])


def plane_send(parts):
    return [parts[0]] + [exchange(parts[k], k) for k in range(1, PLANE)]


def bit(level):
    _, z = place()
    return lax.rem(lax.div(z, 1 << level), 2)


def half(side, rows):
    return pl.ds(pl.multiple_of(side * rows, 8), rows)


def total_kernel(level, *refs):
    parts, outs = refs[:-2], refs[-2:]
    rows = outs[0].shape[0]
    side = bit(level)
    for out, at in zip(outs, (half(side, rows), half(1 - side, rows))):
        total = parts[0][at, :]
        for part in parts[1:]:
            total = total + part[at, :]
        out[...] = total


def sum_kernel(*refs):
    total = refs[0][...]
    for part in refs[1:-1]:
        total = total + part[...]
    refs[-1][...] = total


def first(level, reverse):
    later = bit(level).astype(jnp.float32)
    return (1.0 - later, later) if reverse else (later, 1.0 - later)


def edge_kernel(level, reverse, other, mine, theirs, to_me, to_partner):
    entering = other[...] * first(level + 1, reverse)[0]
    before_me, before_partner = first(level, reverse)
    to_me[...] = entering + theirs[...] * before_me
    to_partner[...] = entering + mine[...] * before_partner


def inner_kernel(level, reverse, kept, received, mine, theirs, to_me, to_partner):
    rows = kept.shape[0]
    side = bit(level + 1)
    before_me, before_partner = first(level, reverse)
    for entering, at in ((kept, half(side, rows)), (received, half(1 - side, rows))):
        to_me[at, :] = entering[...] + theirs[at, :] * before_me
        to_partner[at, :] = entering[...] + mine[at, :] * before_partner


def spread_kernel(reverse, kept, received, *refs):
    parts, outs = refs[:PLANE], refs[PLANE:]
    p, _ = place()
    rows = kept.shape[0]
    side = bit(0)
    for base, at in ((kept, half(side, rows)), (received, half(1 - side, rows))):
        held = [part[at, :] for part in parts]
        for k in range(PLANE):
            target = p ^ k
            total = base[...]
            for j in range(PLANE):
                source = p ^ j
                before = source > target if reverse else source < target
                total = total + held[j] * weight(before)
            outs[k][at, :] = total


def line_steps(run, parts, reverse, level=0):
    levels = (lax.axis_size("seq") // PLANE).bit_length() - 1
    distance = PLANE << level
    rows = parts[0].shape[0] // 2
    mine, send = run(functools.partial(total_kernel, level), [f32(rows, HEAD_DIM)] * 2, *parts)
    theirs = exchange(send, distance)
    yield
    if level == levels - 2:
        (total,) = run(sum_kernel, [f32(rows, HEAD_DIM)], mine, theirs)
        entering = (exchange(total, 2 * distance),)
        body = edge_kernel
        yield
    else:
        entering = yield from line_steps(run, (mine, theirs), reverse, level + 1)
        body = inner_kernel
    kept, send = run(
        functools.partial(body, level, reverse), [f32(rows, HEAD_DIM)] * 2, *entering, mine, theirs
    )
    received = exchange(send, distance)
    yield
    return kept, received


def scan_steps(run, parts, reverse, results):
    parts = plane_send(parts)
    yield
    kept, received = yield from line_steps(run, parts, reverse)
    rows = parts[0].shape[0]
    outs = run(
        functools.partial(spread_kernel, reverse), [f32(rows, HEAD_DIM)] * PLANE, kept, received, *parts
    )
    results.append(plane_send(outs))


def scan_states(run, groups, reverse, fillers, use):
    results = []
    steps = [scan_steps(run, parts, reverse, results) for parts in groups]
    count = 2 * ((lax.axis_size("seq") // PLANE).bit_length() - 1)
    events = [(g / 10 - 1.0, filler) for g, filler in enumerate(fillers)]
    for g, one in enumerate(steps):
        next(one)
        behind = 0.5 + 1.2 * g if g else 0.0
        events += [(behind + step, functools.partial(next, one, None)) for step in range(count)]
        events.append((behind + count + 1, lambda g=g: use(g, results[g])))
    for _, event in sorted(events, key=lambda e: e[0]):
        event()


def fetch(first, sources, targets, sems):
    here = pl.ds(first * HEAD_DIM, targets[0].shape[1])
    copies = [
        pltpu.make_async_copy(source.at[:, here], target, sems.at[i])
        for i, (source, target) in enumerate(zip(sources, targets, strict=True))
    ]
    for copy in copies:
        copy.start()
    for copy in copies:
        copy.wait()


def state_kernel(first, count, keys, values, *refs):
    outs, (left, right, sems) = refs[:PLANE], refs[PLANE:]
    p, _ = place()
    fetch(first, (keys, values), (left, right), sems)
    for k in range(PLANE):
        for j in range(count):
            at = columns((p ^ k) * count + j)
            outs[k][pl.ds(j * HEAD_DIM, HEAD_DIM), :] = dot(left[:, at], right[:, at], CONTRACT_ROWS)


def local_kernel(first, scale, queries, keys, values, weights, inner, q, k, v, sems):
    fetch(first, (queries, keys, values), (q, k, v), sems)
    mask = causal(q.shape[0])
    for h in range(inner.shape[1] // HEAD_DIM):
        at = columns(h)
        scores = dot(q[:, at], k[:, at], CONTRACT_COLUMNS) * scale
        w = jnp.where(mask, scores, 0.0).astype(jnp.bfloat16)
        weights[:, at] = w
        inner[:, at] = dot(w, v[:, at])


def attend_kernel(first, count, scale, queries, inner, cotangent, gain, *refs):
    parts, (attended, prefix_low, stats) = refs[:PLANE], refs[-3:]
    earlier = refs[PLANE:-3]
    p, _ = place()
    squares, cross = (earlier[0][0], earlier[0][1]) if earlier else (0.0, 0.0)
    for k in range(PLANE):
        for j in range(count):
            h = (p ^ k) * count + j
            at, here = columns(first + h), columns(h)
            low = parts[k][pl.ds(j * HEAD_DIM, HEAD_DIM), :].astype(jnp.bfloat16)
            prefix_low[:, here] = low
            a = inner[:, here] + scale * dot(queries[:, at], low)
            attended[:, here] = a
            scaled = cotangent[:, at].astype(jnp.float32) * gain[:, at]
            squares = squares + a * a
            cross = cross + scaled * a
    stats[0] = squares
    stats[1] = cross


def grad_kernel(first, count, width, queries, cotangent, gain, attended, *refs):
    p, _ = place()
    stats, (grad, *outs) = refs[: -PLANE - 1], refs[-PLANE - 1 :]
    squares, cross = stats[0][0], stats[0][1]
    for other in stats[1:]:
        squares, cross = squares + other[0], cross + other[1]
    inverse_rms = lax.rsqrt(jnp.sum(squares, axis=1, keepdims=True) / width + epsilon)
    cross = jnp.sum(cross, axis=1, keepdims=True) * inverse_rms / width
    for k in range(PLANE):
        for j in range(count):
            h = (p ^ k) * count + j
            at, here = columns(first + h), columns(h)
            normed = attended[:, here] * inverse_rms
            scaled = cotangent[:, at].astype(jnp.float32) * gain[:, at]
            g = ((scaled - normed * cross) * inverse_rms).astype(jnp.bfloat16)
            grad[:, here] = g
            outs[k][pl.ds(j * HEAD_DIM, HEAD_DIM), :] = dot(queries[:, at], g, CONTRACT_ROWS)


def local_grad_kernel(first, scale, queries, keys, values, weights, grad, prefix_low, *refs):
    query_grad, key_inner, value_inner, query_block, sem = refs[-5:]
    mask = causal(queries.shape[0])
    heads = grad.shape[1] // HEAD_DIM
    for h in range(heads):
        at, here = columns(first + h), columns(h)
        g = grad[:, here]
        scores = dot(g, values[:, at], CONTRACT_COLUMNS) * scale
        gw = jnp.where(mask, scores, 0.0).astype(jnp.bfloat16)
        query = dot(gw, keys[:, at]) + scale * dot(g, prefix_low[:, here], CONTRACT_COLUMNS)
        query_block[:, here] = query.astype(jnp.bfloat16)
        key_inner[:, here] = dot(gw, queries[:, at], CONTRACT_ROWS)
        value_inner[:, here] = dot(weights[:, here], g, CONTRACT_ROWS)
    copy = pltpu.make_async_copy(query_block, query_grad.at[:, pl.ds(first * HEAD_DIM, heads * HEAD_DIM)], sem.at[0])
    copy.start()
    copy.wait()


def finish_kernel(first, count, scale, keys, values, key_inner, value_inner, *refs):
    parts, (key_grad, value_grad, key_block, value_block, sems) = refs[:PLANE], refs[-5:]
    p, _ = place()
    copies = []
    for k in range(PLANE):
        owner = (p ^ k) * count
        for j in range(count):
            at, here = columns(first + owner + j), columns(owner + j)
            low = parts[k][pl.ds(j * HEAD_DIM, HEAD_DIM), :].astype(jnp.bfloat16)
            key = key_inner[:, here] + scale * dot(values[:, at], low, CONTRACT_COLUMNS)
            key_block[:, here] = key.astype(jnp.bfloat16)
            value = value_inner[:, here] + scale * dot(keys[:, at], low)
            value_block[:, here] = value.astype(jnp.bfloat16)
        for i, (block, result) in enumerate(((key_block, key_grad), (value_block, value_grad))):
            copies.append(
                pltpu.make_async_copy(
                    block.at[:, columns(owner, count)],
                    result.at[:, columns(first + owner, count)],
                    sems.at[2 * k + i],
                )
            )
            copies[-1].start()
    for copy in copies:
        copy.wait()


def per_device(queries, keys, values, cotangent, gain):
    tokens, width = queries.shape
    ways = lax.axis_size("head")
    scale = HEAD_DIM ** (-0.5)
    gain = gain[None, :]
    groups = split_heads(width // HEAD_DIM)
    shares = [PLANE * count * HEAD_DIM for _, count in groups]
    states_of = [[f32(count * HEAD_DIM, HEAD_DIM)] * PLANE for _, count in groups]
    final = len(groups) - 1
    run = Chain()

    def block(g):
        return pltpu.VMEM((tokens, shares[g]), jnp.bfloat16)

    with jax.named_scope("state"):
        states = []
        for g, (first, count) in enumerate(groups):
            states.append(
                run(
                    functools.partial(state_kernel, first, count),
                    states_of[g], keys, values,
                    hbm_args=(0, 1), scratch=[block(g)] * 2 + [pltpu.SemaphoreType.DMA((2,))],
                    mib=16 if g else 54,
                )
            )
            run.last = states[-1][0]

    local, attended, local_grads, ends = [], [], [], []

    def run_local(g):
        local.append(
            run(
                functools.partial(local_kernel, groups[g][0], scale),
                [bf16(tokens, shares[g]), f32(tokens, shares[g])],
                queries, keys, values,
                hbm_args=(0, 1, 2), scratch=[block(g)] * 3 + [pltpu.SemaphoreType.DMA((3,))],
            )
        )

    def attend(g, prefix):
        attended.append(
            run(
                functools.partial(attend_kernel, *groups[g], scale),
                [f32(tokens, shares[g]), bf16(HEAD_DIM, shares[g]), f32(2, tokens, HEAD_DIM)],
                queries, local[g][1], cotangent, gain, *prefix, *[a[2] for a in attended[-1:]],
                flops=1 if g == final else HIDDEN,
            )
        )

    with jax.named_scope("prefix"):
        scan_states(run, states, False, [functools.partial(run_local, g) for g in range(final + 1)], attend)
    with jax.named_scope("statistics"):
        stats = [attended[-1][2]]
        for k in range(1, ways):
            stats.append(lax.ppermute(stats[0], "head", [(h, (h + k) % ways) for h in range(ways)]))
    with jax.named_scope("grad"):
        grads = [
            run(
                functools.partial(grad_kernel, first, count, width * ways),
                [bf16(tokens, shares[g])] + states_of[g],
                queries, cotangent, gain, attended[g][0], *stats,
            )
            for g, (first, count) in enumerate(groups)
        ]

    def run_local_grad(g):
        earlier = [r[0] for r in local_grads[-1:]]
        local_grads.append(
            run(
                functools.partial(local_grad_kernel, groups[g][0], scale),
                [bf16(tokens, width), f32(tokens, shares[g]), f32(tokens, shares[g])],
                queries, keys, values, local[g][0], grads[g][0], attended[g][1], *earlier,
                hbm_args=(6,), hbm_outs=1, aliases={6: 0} if earlier else {},
                scratch=[block(g), pltpu.SemaphoreType.DMA((1,))],
            )
        )

    def finish(g, suffix):
        at = 4 + PLANE
        earlier = ends[-1] if ends else []
        ends.append(
            run(
                functools.partial(finish_kernel, *groups[g], scale),
                [bf16(tokens, width)] * 2,
                keys, values, local_grads[g][1], local_grads[g][2], *suffix, *earlier,
                flops=1 if g == final else HIDDEN,
                hbm_args=(at, at + 1), hbm_outs=2, aliases={at: 0, at + 1: 1} if earlier else {},
                scratch=[block(g), block(g), pltpu.SemaphoreType.DMA((2 * PLANE,))],
            )
        )

    with jax.named_scope("suffix"):
        scan_states(
            run, [g[1:] for g in grads], True, [functools.partial(run_local_grad, g) for g in range(final + 1)], finish
        )
    return local_grads[-1][0], *ends[-1]


def solution(mesh):
    return jax.shard_map(
        per_device,
        mesh=mesh,
        in_specs=(P("seq", "head"), P("seq", "head"), P("seq", "head"), P("seq", "head"), P("head")),
        out_specs=(P("seq", "head"), P("seq", "head"), P("seq", "head")),
        check_vma=False,
    )
```

```python
import functools

import jax
import jax.numpy as jnp
from jax import lax
from jax.experimental import pallas as pl
from jax.experimental.pallas import tpu as pltpu
from jax.sharding import PartitionSpec as P

HEAD_DIM = 128
GROUPS = 2
HIDDEN = 4 * 10**9
PLANE = 4

epsilon = 1e-05

CONTRACT_ROWS = (((0,), (0,)), ((), ()))
CONTRACT_COLUMNS = (((1,), (1,)), ((), ()))


def dot(a, b, dims=(((1,), (0,)), ((), ()))):
    return lax.dot_general(a, b, dims, preferred_element_type=jnp.float32)


class Chain:
    def __init__(self):
        self.last = None

    def __call__(self, body, outs, *args, flops=1, hbm_args=(), hbm_outs=0, aliases=None, scratch=(), mib=16):
        specs = [pl.BlockSpec(memory_space=pltpu.HBM if i in hbm_args else pltpu.VMEM) for i in range(len(args))]
        kernel, operands, count = body, args, len(args)
        if self.last is not None and not any(self.last is arg for arg in args):
            specs, operands = specs + [pl.BlockSpec(memory_space=pl.ANY)], (*args, self.last)

            def kernel(*refs):
                body(*refs[:count], *refs[count + 1 :])

        results = pl.pallas_call(
            kernel,
            out_shape=outs,
            in_specs=specs,
            out_specs=[
                pl.BlockSpec(memory_space=pltpu.HBM if i < hbm_outs else pltpu.VMEM) for i in range(len(outs))
            ],
            scratch_shapes=scratch,
            input_output_aliases=aliases or {},
            cost_estimate=pl.CostEstimate(flops=flops, bytes_accessed=1, transcendentals=0),
            compiler_params=pltpu.CompilerParams(vmem_limit_bytes=mib * 1024 * 1024),
        )(*operands)
        self.last = results[-1]
        return list(results)


def f32(*shape):
    return jax.ShapeDtypeStruct(shape, jnp.float32)


def bf16(*shape):
    return jax.ShapeDtypeStruct(shape, jnp.bfloat16)


def place():
    me = lax.axis_index("seq")
    return lax.rem(me, PLANE), lax.div(me, PLANE)


def weight(condition):
    return jnp.where(condition, 1.0, 0.0).astype(jnp.float32)


def columns(head, count=1):
    return pl.ds(pl.multiple_of(head * HEAD_DIM, HEAD_DIM), count * HEAD_DIM)


def split_heads(heads):
    per_owner = heads // PLANE
    groups = min(GROUPS, per_owner)
    sizes = [per_owner // groups + (g < per_owner % groups) for g in range(groups)]
    return [(PLANE * sum(sizes[:g]), sizes[g]) for g in range(groups)]


def causal(tokens):
    rows_index = lax.broadcasted_iota(jnp.int32, (tokens, tokens), 0)
    cols_index = lax.broadcasted_iota(jnp.int32, (tokens, tokens), 1)
    return rows_index >= cols_index


def exchange(value, distance):
    n = lax.axis_size("seq")
    return lax.ppermute(value, "seq", [(s, s ^ distance) for s in range(n)])


def plane_send(parts):
    return [parts[0]] + [exchange(parts[k], k) for k in range(1, PLANE)]


def bit(level):
    _, z = place()
    return lax.rem(lax.div(z, 1 << level), 2)


def half(side, rows):
    return pl.ds(pl.multiple_of(side * rows, 8), rows)


def total_kernel(level, *refs):
    parts, outs = refs[:-2], refs[-2:]
    rows = outs[0].shape[0]
    side = bit(level)
    for out, at in zip(outs, (half(side, rows), half(1 - side, rows))):
        total = parts[0][at, :]
        for part in parts[1:]:
            total = total + part[at, :]
        out[...] = total


def sum_kernel(*refs):
    total = refs[0][...]
    for part in refs[1:-1]:
        total = total + part[...]
    refs[-1][...] = total


def first(level, reverse):
    later = bit(level).astype(jnp.float32)
    return (1.0 - later, later) if reverse else (later, 1.0 - later)


def edge_kernel(level, reverse, other, mine, theirs, to_me, to_partner):
    entering = other[...] * first(level + 1, reverse)[0]
    before_me, before_partner = first(level, reverse)
    to_me[...] = entering + theirs[...] * before_me
    to_partner[...] = entering + mine[...] * before_partner


def inner_kernel(level, reverse, kept, received, mine, theirs, to_me, to_partner):
    rows = kept.shape[0]
    side = bit(level + 1)
    before_me, before_partner = first(level, reverse)
    for entering, at in ((kept, half(side, rows)), (received, half(1 - side, rows))):
        to_me[at, :] = entering[...] + theirs[at, :] * before_me
        to_partner[at, :] = entering[...] + mine[at, :] * before_partner


def spread_kernel(reverse, kept, received, *refs):
    parts, outs = refs[:PLANE], refs[PLANE:]
    p, _ = place()
    rows = kept.shape[0]
    side = bit(0)
    for base, at in ((kept, half(side, rows)), (received, half(1 - side, rows))):
        held = [part[at, :] for part in parts]
        for k in range(PLANE):
            target = p ^ k
            total = base[...]
            for j in range(PLANE):
                source = p ^ j
                before = source > target if reverse else source < target
                total = total + held[j] * weight(before)
            outs[k][at, :] = total


def line_steps(run, parts, reverse, level=0):
    levels = (lax.axis_size("seq") // PLANE).bit_length() - 1
    distance = PLANE << level
    rows = parts[0].shape[0] // 2
    mine, send = run(functools.partial(total_kernel, level), [f32(rows, HEAD_DIM)] * 2, *parts)
    theirs = exchange(send, distance)
    yield
    if level == levels - 2:
        (total,) = run(sum_kernel, [f32(rows, HEAD_DIM)], mine, theirs)
        entering = (exchange(total, 2 * distance),)
        body = edge_kernel
        yield
    else:
        entering = yield from line_steps(run, (mine, theirs), reverse, level + 1)
        body = inner_kernel
    kept, send = run(
        functools.partial(body, level, reverse), [f32(rows, HEAD_DIM)] * 2, *entering, mine, theirs
    )
    received = exchange(send, distance)
    yield
    return kept, received


def scan_steps(run, parts, reverse, results):
    parts = plane_send(parts)
    yield
    kept, received = yield from line_steps(run, parts, reverse)
    rows = parts[0].shape[0]
    outs = run(
        functools.partial(spread_kernel, reverse), [f32(rows, HEAD_DIM)] * PLANE, kept, received, *parts
    )
    results.append(plane_send(outs))


def scan_states(run, groups, reverse, fillers, use):
    results = []
    steps = [scan_steps(run, parts, reverse, results) for parts in groups]
    count = 2 * ((lax.axis_size("seq") // PLANE).bit_length() - 1)
    events = []
    for g, one in enumerate(steps):
        next(one)
        behind = 0.5 + 1.2 * g if g else 0.0
        last = g > 0 and g == len(steps) - 1
        events.append((behind + count + 0.5 if last else g / 10 - 1.0, fillers[g]))
        events += [(behind + step, functools.partial(next, one, None)) for step in range(count)]
        events.append((behind + count + 1, lambda g=g: use(g, results[g])))
    for _, event in sorted(events, key=lambda e: e[0]):
        event()


def fetch(first, sources, targets, sems):
    here = pl.ds(first * HEAD_DIM, targets[0].shape[1])
    copies = [
        pltpu.make_async_copy(source.at[:, here], target, sems.at[i])
        for i, (source, target) in enumerate(zip(sources, targets, strict=True))
    ]
    for copy in copies:
        copy.start()
    for copy in copies:
        copy.wait()


def state_kernel(first, count, keys, values, *refs):
    outs, (left, right, sems) = refs[:PLANE], refs[PLANE:]
    p, _ = place()
    fetch(first, (keys, values), (left, right), sems)
    for k in range(PLANE):
        for j in range(count):
            at = columns((p ^ k) * count + j)
            outs[k][pl.ds(j * HEAD_DIM, HEAD_DIM), :] = dot(left[:, at], right[:, at], CONTRACT_ROWS)


def local_kernel(first, scale, queries, keys, values, weights, inner, q, k, v, sems):
    fetch(first, (queries, keys, values), (q, k, v), sems)
    mask = causal(q.shape[0])
    for h in range(inner.shape[1] // HEAD_DIM):
        at = columns(h)
        scores = dot(q[:, at], k[:, at], CONTRACT_COLUMNS) * scale
        w = jnp.where(mask, scores, 0.0).astype(jnp.bfloat16)
        weights[:, at] = w
        inner[:, at] = dot(w, v[:, at])


def attend_kernel(first, count, scale, queries, inner, cotangent, gain, *refs):
    parts, (attended, prefix_low, stats) = refs[:PLANE], refs[-3:]
    earlier = refs[PLANE:-3]
    p, _ = place()
    squares, cross = (earlier[0][0], earlier[0][1]) if earlier else (0.0, 0.0)
    for k in range(PLANE):
        for j in range(count):
            h = (p ^ k) * count + j
            at, here = columns(first + h), columns(h)
            low = parts[k][pl.ds(j * HEAD_DIM, HEAD_DIM), :].astype(jnp.bfloat16)
            prefix_low[:, here] = low
            a = inner[:, here] + scale * dot(queries[:, at], low)
            attended[:, here] = a
            scaled = cotangent[:, at].astype(jnp.float32) * gain[:, at]
            squares = squares + a * a
            cross = cross + scaled * a
    stats[0] = squares
    stats[1] = cross


def grad_kernel(first, count, width, queries, cotangent, gain, attended, *refs):
    p, _ = place()
    stats, (grad, *outs) = refs[: -PLANE - 1], refs[-PLANE - 1 :]
    squares, cross = stats[0][0], stats[0][1]
    for other in stats[1:]:
        squares, cross = squares + other[0], cross + other[1]
    inverse_rms = lax.rsqrt(jnp.sum(squares, axis=1, keepdims=True) / width + epsilon)
    cross = jnp.sum(cross, axis=1, keepdims=True) * inverse_rms / width
    for k in range(PLANE):
        for j in range(count):
            h = (p ^ k) * count + j
            at, here = columns(first + h), columns(h)
            normed = attended[:, here] * inverse_rms
            scaled = cotangent[:, at].astype(jnp.float32) * gain[:, at]
            g = ((scaled - normed * cross) * inverse_rms).astype(jnp.bfloat16)
            grad[:, here] = g
            outs[k][pl.ds(j * HEAD_DIM, HEAD_DIM), :] = dot(queries[:, at], g, CONTRACT_ROWS)


def local_grad_kernel(first, scale, queries, keys, values, weights, grad, prefix_low, *refs):
    query_grad, key_inner, value_inner, query_block, sem = refs[-5:]
    mask = causal(queries.shape[0])
    heads = grad.shape[1] // HEAD_DIM
    for h in range(heads):
        at, here = columns(first + h), columns(h)
        g = grad[:, here]
        scores = dot(g, values[:, at], CONTRACT_COLUMNS) * scale
        gw = jnp.where(mask, scores, 0.0).astype(jnp.bfloat16)
        query = dot(gw, keys[:, at]) + scale * dot(g, prefix_low[:, here], CONTRACT_COLUMNS)
        query_block[:, here] = query.astype(jnp.bfloat16)
        key_inner[:, here] = dot(gw, queries[:, at], CONTRACT_ROWS)
        value_inner[:, here] = dot(weights[:, here], g, CONTRACT_ROWS)
    copy = pltpu.make_async_copy(query_block, query_grad.at[:, pl.ds(first * HEAD_DIM, heads * HEAD_DIM)], sem.at[0])
    copy.start()
    copy.wait()


def finish_kernel(first, count, scale, keys, values, key_inner, value_inner, *refs):
    parts, (key_grad, value_grad, key_block, value_block, sems) = refs[:PLANE], refs[-5:]
    p, _ = place()
    copies = []
    for k in range(PLANE):
        owner = (p ^ k) * count
        for j in range(count):
            at, here = columns(first + owner + j), columns(owner + j)
            low = parts[k][pl.ds(j * HEAD_DIM, HEAD_DIM), :].astype(jnp.bfloat16)
            key = key_inner[:, here] + scale * dot(values[:, at], low, CONTRACT_COLUMNS)
            key_block[:, here] = key.astype(jnp.bfloat16)
            value = value_inner[:, here] + scale * dot(keys[:, at], low)
            value_block[:, here] = value.astype(jnp.bfloat16)
        for i, (block, result) in enumerate(((key_block, key_grad), (value_block, value_grad))):
            copies.append(
                pltpu.make_async_copy(
                    block.at[:, columns(owner, count)],
                    result.at[:, columns(first + owner, count)],
                    sems.at[2 * k + i],
                )
            )
            copies[-1].start()
    for copy in copies:
        copy.wait()


def per_device(queries, keys, values, cotangent, gain):
    tokens, width = queries.shape
    ways = lax.axis_size("head")
    scale = HEAD_DIM ** (-0.5)
    gain = gain[None, :]
    groups = split_heads(width // HEAD_DIM)
    shares = [PLANE * count * HEAD_DIM for _, count in groups]
    states_of = [[f32(count * HEAD_DIM, HEAD_DIM)] * PLANE for _, count in groups]
    final = len(groups) - 1
    run = Chain()

    def block(g):
        return pltpu.VMEM((tokens, shares[g]), jnp.bfloat16)

    with jax.named_scope("state"):
        states = []
        for g, (first, count) in enumerate(groups):
            states.append(
                run(
                    functools.partial(state_kernel, first, count),
                    states_of[g], keys, values,
                    hbm_args=(0, 1), scratch=[block(g)] * 2 + [pltpu.SemaphoreType.DMA((2,))],
                    mib=16 if g else 54,
                )
            )
            run.last = states[-1][0]

    local, attended, local_grads, ends = [], [], [], []

    def run_local(g):
        local.append(
            run(
                functools.partial(local_kernel, groups[g][0], scale),
                [bf16(tokens, shares[g]), f32(tokens, shares[g])],
                queries, keys, values,
                hbm_args=(0, 1, 2), scratch=[block(g)] * 3 + [pltpu.SemaphoreType.DMA((3,))],
            )
        )

    def attend(g, prefix):
        attended.append(
            run(
                functools.partial(attend_kernel, *groups[g], scale),
                [f32(tokens, shares[g]), bf16(HEAD_DIM, shares[g]), f32(2, tokens, HEAD_DIM)],
                queries, local[g][1], cotangent, gain, *prefix, *[a[2] for a in attended[-1:]],
                flops=1 if g == final else HIDDEN,
            )
        )

    with jax.named_scope("prefix"):
        scan_states(run, states, False, [functools.partial(run_local, g) for g in range(final + 1)], attend)
    with jax.named_scope("statistics"):
        stats = [attended[-1][2]]
        for k in range(1, ways):
            stats.append(lax.ppermute(stats[0], "head", [(h, (h + k) % ways) for h in range(ways)]))
    with jax.named_scope("grad"):
        grads = [
            run(
                functools.partial(grad_kernel, first, count, width * ways),
                [bf16(tokens, shares[g])] + states_of[g],
                queries, cotangent, gain, attended[g][0], *stats,
            )
            for g, (first, count) in enumerate(groups)
        ]

    def run_local_grad(g):
        earlier = [r[0] for r in local_grads[-1:]]
        local_grads.append(
            run(
                functools.partial(local_grad_kernel, groups[g][0], scale),
                [bf16(tokens, width), f32(tokens, shares[g]), f32(tokens, shares[g])],
                queries, keys, values, local[g][0], grads[g][0], attended[g][1], *earlier,
                hbm_args=(6,), hbm_outs=1, aliases={6: 0} if earlier else {},
                scratch=[block(g), pltpu.SemaphoreType.DMA((1,))],
            )
        )

    def finish(g, suffix):
        at = 4 + PLANE
        earlier = ends[-1] if ends else []
        ends.append(
            run(
                functools.partial(finish_kernel, *groups[g], scale),
                [bf16(tokens, width)] * 2,
                keys, values, local_grads[g][1], local_grads[g][2], *suffix, *earlier,
                flops=1 if g == final else HIDDEN,
                hbm_args=(at, at + 1), hbm_outs=2, aliases={at: 0, at + 1: 1} if earlier else {},
                scratch=[block(g), block(g), pltpu.SemaphoreType.DMA((2 * PLANE,))],
            )
        )

    with jax.named_scope("suffix"):
        scan_states(
            run, [g[1:] for g in grads], True, [functools.partial(run_local_grad, g) for g in range(final + 1)], finish
        )
    return local_grads[-1][0], *ends[-1]


def solution(mesh):
    return jax.shard_map(
        per_device,
        mesh=mesh,
        in_specs=(P("seq", "head"), P("seq", "head"), P("seq", "head"), P("seq", "head"), P("head")),
        out_specs=(P("seq", "head"), P("seq", "head"), P("seq", "head")),
        check_vma=False,
    )
```
